1024 devices in a mesh: dp: 32 (over x, y_hi), tensor: 32 (over z, y_lo, core).
Axes of the slice: x: 8, y: 8 (y_hi: 4, y_lo: 2; y = y_hi * 2 + y_lo), z: 8, core: 2. Of those that a mesh axis runs over, the one named last changes fastest.
Arguments:
- tokens: bfloat16 [512, 18432], P('tensor', 'dp'), may hold values from -6 to 6
- up_weight: bfloat16 [18432, 36864], P('dp', 'tensor'), may hold values from -0.078125 to 0.078125
- down_weight: bfloat16 [36864, 18432], P('tensor', 'dp'), may hold values from -0.078125 to 0.078125
- keep_bits: int32 [512, 18432], P('tensor', 'dp'), may hold values 0 or 1
- prior_scale: float32 [1], replicated, may hold values from 60 to 200
Outputs:
- scaled: bfloat16 [512, 18432], P('tensor', 'dp')
- amax: float32 [1], replicated
The draws below stay inside these ranges and needn't reach their ends.
All inputs are finite; a program needn't handle non-finite values. No bound on the sum of `keep_bits` on one device may be relied on, other than what follows from the above.
Results may differ from the reference program's by a relative error of at most 0.0045.
Values may be sent and summed in bfloat16 or wider, within the bound.
No kernel may reach another device: no remote copies, remote signals or barrier semaphores. Data moves between devices by JAX's collectives and lax.ppermute only.
A program may use at most 32 MiB of HBM per device.

```python
import math
import jax
import jax.numpy as jnp

D = 18432
FF = 36864
TOKENS = 512


def plant(drawn, stream_key, low, top_value):
    place = [jax.random.randint(jax.random.fold_in(stream_key, axis), (), 0, length) for axis, length in enumerate(drawn.shape)]
    main_axis = drawn.shape.index(max(drawn.shape))
    neighbour = place[:main_axis] + [(place[main_axis] + 1) % drawn.shape[main_axis]] + place[main_axis + 1:]
    return drawn.at[tuple(place)].set(low).at[tuple(neighbour)].set(top_value)


def with_spikes(values, stream_key, source, target, blocks, factor):
    owner, partner = [(jnp.arange(values.shape[dim]) // (values.shape[dim] // blocks)).reshape([-1 if axis == dim else 1 for axis in range(values.ndim)]) for dim in (source, target)]
    chosen = jax.random.permutation(stream_key, blocks)[partner]
    strong = (owner == chosen) | (owner == (partner + blocks // 2) % blocks)
    return jnp.where(strong, factor * values, values)


def steps_of(own_key, dims, cuts, low, largest):
    level = 1.0
    for axis_at, shards_of in cuts:
        draws = jax.random.uniform(jax.random.fold_in(jax.random.fold_in(own_key, 6), axis_at), (shards_of,), jnp.float32, low / len(cuts), largest / len(cuts))
        level = level * jnp.repeat(jnp.exp(draws), dims[axis_at] // shards_of).reshape((-1,) + (1,) * (len(dims) - 1 - axis_at))
    return level


def scatter_about(own_key, shape, deviation, most, split=(), dtype=jnp.bfloat16):
    values = deviation * jax.random.normal(own_key, shape, jnp.float32)
    if split:
        values = values * steps_of(own_key, shape, split, -0.22, 0.18)
    return jnp.clip(values, -most, most).astype(dtype)


def bell_draw_with(key, shape, width, limit, pieces, heavy, kind=jnp.bfloat16):
    entries = width * jax.random.normal(key, shape, jnp.float32)
    if pieces:
        entries = entries * steps_of(key, shape, pieces, -0.22, 0.18)
    return jnp.clip(with_spikes(entries, jax.random.fold_in(key, 3), *heavy), -limit, limit).astype(kind)


def setup_inputs(seed: int = 0) -> dict:
    key_of = jax.random.split(jax.random.key(seed), 6)
    tokens = scatter_about(key_of[0], (TOKENS, D), 1.0, 6.0, ((0, 32), (1, 32)))
    up_weight = bell_draw_with(key_of[1], (D, FF), D ** -0.5, 0.078125, ((0, 32), (1, 32)), (0, 1, 32, 2.75))
    down_weight = bell_draw_with(key_of[2], (FF, D), (FF // 2) ** -0.5, 0.078125, ((0, 32), (1, 32)), (0, 1, 32, 2.75))
    keep_bits = plant((jax.random.randint(key_of[3], (TOKENS, D), 0, 10) < 9).astype(jnp.int32), jax.random.fold_in(key_of[3], 1), 0, 1)
    prior_scale = jnp.clip(jnp.exp(jax.random.uniform(key_of[4], (1,), jnp.float32, math.log(60.0), math.log(200.0))), 60.0, 200.0)
    return dict(tokens=tokens, up_weight=up_weight, down_weight=down_weight, keep_bits=keep_bits, prior_scale=prior_scale)


def reference(tokens, up_weight, down_weight, keep_bits, prior_scale):
    hidden = jnp.dot(tokens, up_weight, preferred_element_type=jnp.float32)
    positive = jnp.maximum(hidden, 0.0)
    active = (positive * positive).astype(jnp.bfloat16)
    mlp_out = jnp.dot(active, down_weight, preferred_element_type=jnp.float32)
    combined = tokens.astype(jnp.float32) + keep_bits.astype(jnp.float32) * mlp_out / 0.9
    amax = jnp.max(jnp.abs(combined)).reshape(1)
    scaled = jnp.clip(combined * prior_scale[0], -448.0, 448.0).astype(jnp.bfloat16)
    return scaled, amax
```

```python
import jax
import jax.numpy as jnp
from jax import lax
from jax.sharding import Mesh, PartitionSpec as P

DP = ("x", "yh")
TENSOR = ("z", "yl", "core")
LIFT = 128.0


def exchange(blocks, axes):
    return lax.all_to_all(blocks, axes, split_axis=0, concat_axis=0, tiled=True)


def gather(block, axes, n):
    spread = exchange(jnp.broadcast_to(block, (n,) + block.shape), axes)
    return spread.reshape((n * block.shape[0],) + block.shape[1:])


def max_over(value, axes, n):
    return jnp.max(exchange(jnp.full((n, 1, 128), value), axes))


def body(tokens, up_weight, down_weight, keep_bits, prior_scale):
    rows, width = tokens.shape
    shards = up_weight.shape[1]
    half = gather(tokens, ("z", "yl"), 16)
    gathered = lax.all_gather(half, "core", axis=0, tiled=True)
    hidden_part = jnp.dot(gathered, up_weight, preferred_element_type=jnp.float32)
    hidden_part = (hidden_part * LIFT).astype(jnp.float16).reshape(32, rows, shards)
    hidden = jnp.sum(exchange(hidden_part, DP).astype(jnp.float32), axis=0) * (1.0 / LIFT)
    positive = jnp.maximum(hidden, 0.0)
    active = gather((positive * positive).astype(jnp.bfloat16), DP, 32)
    out_part = jnp.dot(active, down_weight, preferred_element_type=jnp.float32)
    out_part = lax.psum_scatter(out_part, "core", scatter_dimension=0, tiled=True)
    out_part = out_part.astype(jnp.bfloat16).reshape(16, rows, width)
    mlp_out = jnp.sum(exchange(out_part, ("z", "yl")).astype(jnp.float32), axis=0)
    combined = tokens.astype(jnp.float32) + keep_bits.astype(jnp.float32) * mlp_out / 0.9
    amax = max_over(max_over(jnp.max(jnp.abs(combined)), DP, 32), TENSOR, 32).reshape(1)
    scaled = jnp.clip(combined * prior_scale[0], -448.0, 448.0).astype(jnp.bfloat16)
    return (scaled, amax)


def solution(mesh):
    fine = Mesh(mesh.devices.reshape(8, 4, 8, 2, 2), DP + TENSOR)
    return jax.shard_map(
        body,
        mesh=fine,
        in_specs=(P(TENSOR, DP), P(DP, TENSOR), P(TENSOR, DP), P(TENSOR, DP), P()),
        out_specs=(P(TENSOR, DP), P()),
        check_vma=False,
    )
```

```python
import jax
import jax.numpy as jnp
from jax import lax
from jax.experimental.layout import Layout, with_layout_constraint
from jax.sharding import Mesh, PartitionSpec as P

DP = ("x", "yh")
TENSOR = ("z", "yl", "core")
LIFT = 128.0
ROW_MAJOR = Layout(major_to_minor=(0, 1))


def exchange(blocks, axes):
    return lax.all_to_all(blocks, axes, split_axis=0, concat_axis=0, tiled=True)


def gather(block, axes, n):
    spread = exchange(jnp.broadcast_to(block, (n,) + block.shape), axes)
    return spread.reshape((n * block.shape[0],) + block.shape[1:])


def max_over(value, axes, n):
    return jnp.max(exchange(jnp.full((n, 1, 128), value), axes))


def body(tokens, up_weight, down_weight, keep_bits, prior_scale):
    rows, width = tokens.shape
    shards = up_weight.shape[1]
    half = gather(tokens, ("z", "yl"), 16)
    gathered = lax.all_gather(half, "core", axis=0, tiled=True)
    hidden_part = jnp.dot(gathered, up_weight, preferred_element_type=jnp.float32)
    hidden_part = (hidden_part * LIFT).astype(jnp.float16).reshape(32, rows, shards)
    hidden = jnp.sum(exchange(hidden_part, DP).astype(jnp.float32), axis=0) * (1.0 / LIFT)
    positive = jnp.maximum(hidden, 0.0)
    active = gather((positive * positive).astype(jnp.bfloat16), DP, 32)
    out_part = jnp.dot(active, down_weight, preferred_element_type=jnp.float32)
    out_part = with_layout_constraint(out_part, ROW_MAJOR)
    pair = exchange(out_part.reshape(2, 16, rows, width), "core")
    out_part = (pair[0] + pair[1]).astype(jnp.bfloat16)
    mlp_out = jnp.sum(exchange(out_part, ("z", "yl")).astype(jnp.float32), axis=0)
    combined = tokens.astype(jnp.float32) + keep_bits.astype(jnp.float32) * mlp_out / 0.9
    amax = max_over(max_over(jnp.max(jnp.abs(combined)), DP, 32), TENSOR, 32).reshape(1)
    scaled = jnp.clip(combined * prior_scale[0], -448.0, 448.0).astype(jnp.bfloat16)
    return (scaled, amax)


def solution(mesh):
    fine = Mesh(mesh.devices.reshape(8, 4, 8, 2, 2), DP + TENSOR)
    return jax.shard_map(
        body,
        mesh=fine,
        in_specs=(P(TENSOR, DP), P(DP, TENSOR), P(TENSOR, DP), P(TENSOR, DP), P()),
        out_specs=(P(TENSOR, DP), P()),
        check_vma=False,
    )
```

```python
import jax
import jax.numpy as jnp
from jax import lax
from jax.experimental.layout import Layout, with_layout_constraint
from jax.sharding import Mesh, PartitionSpec as P

DP = ("x", "yh")
TENSOR = ("z", "yl", "core")
LIFT = 128.0
ROW_MAJOR = Layout(major_to_minor=(0, 1))


def exchange(blocks, axes):
    return lax.all_to_all(blocks, axes, split_axis=0, concat_axis=0, tiled=True)


def gather(block, axes, n):
    spread = exchange(jnp.broadcast_to(block, (n,) + block.shape), axes)
    return spread.reshape((n * block.shape[0],) + block.shape[1:])


def max_over(values, axes, n):
    return jnp.max(exchange(jnp.broadcast_to(values, (n,) + values.shape), axes), axis=0)


def body(tokens, up_weight, down_weight, keep_bits, prior_scale):
    rows, width = tokens.shape
    shards = up_weight.shape[1]
    half = gather(tokens, ("z", "yl"), 16)
    gathered = lax.all_gather(half, "core", axis=0, tiled=True)
    hidden_part = jnp.dot(gathered, up_weight, preferred_element_type=jnp.float32)
    hidden_part = (hidden_part * LIFT).astype(jnp.float16).reshape(32, rows, shards)
    hidden = jnp.sum(exchange(hidden_part, ("yh", "x")).astype(jnp.float32), axis=0) * (1.0 / LIFT)
    positive = jnp.maximum(hidden, 0.0)
    active = gather((positive * positive).astype(jnp.bfloat16), "x", 8)
    active = gather(active, "yh", 4)
    out_part = jnp.dot(active, down_weight, preferred_element_type=jnp.float32)
    out_part = with_layout_constraint(out_part, ROW_MAJOR)
    pair = exchange(out_part.reshape(2, 16, rows, width), "core")
    out_part = (pair[0] + pair[1]).astype(jnp.bfloat16)
    mlp_out = jnp.sum(exchange(out_part, ("z", "yl")).astype(jnp.float32), axis=0)
    combined = tokens.astype(jnp.float32) + keep_bits.astype(jnp.float32) * mlp_out / 0.9
    largest = jnp.max(jnp.abs(combined), axis=0, keepdims=True)
    amax = jnp.max(max_over(max_over(largest, DP, 32), TENSOR, 32)).reshape(1)
    scaled = jnp.clip(combined * prior_scale[0], -448.0, 448.0).astype(jnp.bfloat16)
    return (scaled, amax)


def solution(mesh):
    fine = Mesh(mesh.devices.reshape(8, 4, 8, 2, 2), DP + TENSOR)
    return jax.shard_map(
        body,
        mesh=fine,
        in_specs=(P(TENSOR, DP), P(DP, TENSOR), P(TENSOR, DP), P(TENSOR, DP), P()),
        out_specs=(P(TENSOR, DP), P()),
        check_vma=False,
    )
```

```python
import jax
import jax.numpy as jnp
from jax import lax
from jax.experimental.layout import Layout, with_layout_constraint
from jax.sharding import Mesh, PartitionSpec as P

DP = ("x", "yh")
TENSOR = ("z", "yl", "core")
LIFT = 128.0
LOW_LIFT = 16.0
ROW_MAJOR = Layout(major_to_minor=(0, 1))


def exchange(blocks, axes):
    return lax.all_to_all(blocks, axes, split_axis=0, concat_axis=0, tiled=True)


def gather(block, axes, n):
    spread = exchange(jnp.broadcast_to(block, (n,) + block.shape), axes)
    return spread.reshape((n * block.shape[0],) + block.shape[1:])


def max_over(values, axes, n):
    return jnp.max(exchange(jnp.broadcast_to(values, (n,) + values.shape), axes), axis=0)


def body(tokens, up_weight, down_weight, keep_bits, prior_scale):
    rows, width = tokens.shape
    shards = up_weight.shape[1]
    half = gather(tokens, ("z", "yl"), 16)
    gathered = lax.all_gather(half, "core", axis=0, tiled=True)
    hidden_part = jnp.dot(gathered, up_weight, preferred_element_type=jnp.float32)
    hidden_part = (hidden_part * LIFT).astype(jnp.float16).reshape(8, 4 * rows, shards)
    hidden_part = jnp.sum(exchange(hidden_part, "x").astype(jnp.float32), axis=0)
    hidden_part = (hidden_part * (LOW_LIFT / LIFT)).astype(jnp.float16)
    spread = exchange(jnp.broadcast_to(hidden_part, (4,) + hidden_part.shape), "yh")
    hidden = jnp.sum(spread.astype(jnp.float32), axis=0) * (1.0 / LOW_LIFT)
    positive = jnp.maximum(hidden, 0.0)
    active = gather((positive * positive).astype(jnp.bfloat16), "x", 8)
    out_part = jnp.dot(active, down_weight, preferred_element_type=jnp.float32)
    out_part = with_layout_constraint(out_part, ROW_MAJOR)
    pair = exchange(out_part.reshape(2, 16, rows, width), "core")
    out_part = (pair[0] + pair[1]).astype(jnp.bfloat16)
    mlp_out = jnp.sum(exchange(out_part, ("z", "yl")).astype(jnp.float32), axis=0)
    combined = tokens.astype(jnp.float32) + keep_bits.astype(jnp.float32) * mlp_out / 0.9
    largest = jnp.max(jnp.abs(combined), axis=0, keepdims=True)
    amax = jnp.max(max_over(max_over(largest, DP, 32), TENSOR, 32)).reshape(1)
    scaled = jnp.clip(combined * prior_scale[0], -448.0, 448.0).astype(jnp.bfloat16)
    return (scaled, amax)


def solution(mesh):
    fine = Mesh(mesh.devices.reshape(8, 4, 8, 2, 2), DP + TENSOR)
    return jax.shard_map(
        body,
        mesh=fine,
        in_specs=(P(TENSOR, DP), P(DP, TENSOR), P(TENSOR, DP), P(TENSOR, DP), P()),
        out_specs=(P(TENSOR, DP), P()),
        check_vma=False,
    )
```

```python
import jax
import jax.numpy as jnp
from jax import lax
from jax.experimental.layout import Layout, with_layout_constraint
from jax.sharding import Mesh, PartitionSpec as P

DP = ("x", "yh")
TENSOR = ("z", "yl", "core")
LIFT = 128.0
ROW_MAJOR = Layout(major_to_minor=(0, 1))


def exchange(blocks, axes):
    return lax.all_to_all(blocks, axes, split_axis=0, concat_axis=0, tiled=True)


def gather(block, axes, n):
    spread = exchange(jnp.broadcast_to(block, (n,) + block.shape), axes)
    return spread.reshape((n * block.shape[0],) + block.shape[1:])


def max_over(values, axes, n):
    return jnp.max(exchange(jnp.broadcast_to(values, (n,) + values.shape), axes), axis=0)


def lane_maxima(values):
    lanes = 128
    tail = values.shape[1] % lanes
    largest = jnp.max(jnp.pad(values[:, values.shape[1] - tail :], ((0, 0), (0, lanes - tail))), axis=0)
    for low in range(0, values.shape[1] - tail, lanes):
        largest = jnp.maximum(largest, jnp.max(values[:, low : low + lanes], axis=0))
    return largest[None]


def body(tokens, up_weight, down_weight, keep_bits, prior_scale):
    rows, width = tokens.shape
    shards = up_weight.shape[1]
    first, tokens = lax.optimization_barrier((lax.axis_index("core") == 0, tokens))
    half = gather(tokens, ("z", "yl"), 16)
    gathered = lax.all_gather(half, "core", axis=0, tiled=True)
    hidden_part = jnp.dot(gathered, up_weight, preferred_element_type=jnp.float32)
    hidden_part = (hidden_part * LIFT).astype(jnp.float16).reshape(32, rows, shards)
    hidden = jnp.sum(exchange(hidden_part, DP).astype(jnp.float32), axis=0) * (1.0 / LIFT)
    positive = jnp.maximum(hidden, 0.0)
    active = gather((positive * positive).astype(jnp.bfloat16), DP, 32)
    out_part = jnp.dot(active, down_weight, preferred_element_type=jnp.float32)
    out_part = with_layout_constraint(out_part, ROW_MAJOR)
    low, high = out_part[: 16 * rows], out_part[16 * rows :]
    swapped = lax.all_gather(jnp.where(first, high, low).astype(jnp.bfloat16), "core", axis=0)
    other = jnp.where(first, swapped[1], swapped[0]).astype(jnp.float32)
    out_part = (jnp.where(first, low, high) + other).astype(jnp.bfloat16).reshape(16, rows, width)
    mlp_out = jnp.sum(exchange(out_part, ("z", "yl")).astype(jnp.float32), axis=0)
    combined = tokens.astype(jnp.float32) + keep_bits.astype(jnp.float32) * mlp_out / 0.9
    largest = lane_maxima(jnp.abs(combined))
    amax = jnp.max(max_over(max_over(largest, DP, 32), TENSOR, 32)).reshape(1)
    scaled = jnp.clip(combined * prior_scale[0], -448.0, 448.0).astype(jnp.bfloat16)
    return (scaled, amax)


def solution(mesh):
    fine = Mesh(mesh.devices.reshape(8, 4, 8, 2, 2), DP + TENSOR)
    return jax.shard_map(
        body,
        mesh=fine,
        in_specs=(P(TENSOR, DP), P(DP, TENSOR), P(TENSOR, DP), P(TENSOR, DP), P()),
        out_specs=(P(TENSOR, DP), P()),
        check_vma=False,
    )
```

```python
import jax
import jax.numpy as jnp
from jax import lax
from jax.experimental.layout import Layout, with_layout_constraint
from jax.sharding import Mesh, PartitionSpec as P

DP = ("xp", "xh", "yh")
TENSOR = ("z", "yl", "core")
LIKE = ("xp", "yh")
LIFT = 64.0
ROW_MAJOR = Layout(major_to_minor=(0, 1))


def exchange(blocks, axes):
    return lax.all_to_all(blocks, axes, split_axis=0, concat_axis=0, tiled=True)


def gather(block, axes, n):
    spread = exchange(jnp.broadcast_to(block, (n,) + block.shape), axes)
    return spread.reshape((n * block.shape[0],) + block.shape[1:])


def max_over(values, axes, n):
    return jnp.max(exchange(jnp.broadcast_to(values, (n,) + values.shape), axes), axis=0)


def lane_maxima(values):
    lanes = 128
    tail = values.shape[1] % lanes
    largest = jnp.max(jnp.pad(values[:, values.shape[1] - tail :], ((0, 0), (0, lanes - tail))), axis=0)
    for low in range(0, values.shape[1] - tail, lanes):
        largest = jnp.maximum(largest, jnp.max(values[:, low : low + lanes], axis=0))
    return largest[None]


def partner(x, n):
    return (x + 1) % n if x % 2 else (x - 1) % n


def body(tokens, up_weight, down_weight, keep_bits, prior_scale):
    rows, width = tokens.shape
    shards = up_weight.shape[1]
    n = 2 * lax.axis_size("xp")
    blocks = lax.axis_size("z") * lax.axis_size("yl")
    core = lax.axis_index("core")
    first, same, tokens = lax.optimization_barrier((core == 0, core == lax.axis_index("xh"), tokens))
    moves = []
    for x in range(n):
        moves.append((2 * x + x % 2, 2 * x))
        moves.append((2 * x + 1 - x % 2, 2 * partner(x, n) + 1))
    chosen = lax.ppermute(tokens, ("xp", "xh", "core"), moves)
    chosen, up_sent, down_sent = lax.optimization_barrier((chosen, up_weight, down_weight))
    up_other = lax.ppermute(up_sent, ("xp", "xh"), [(x, partner(x, n)) for x in range(n)])
    down_other = lax.ppermute(down_sent, "xh", [(0, 1), (1, 0)])
    half = gather(chosen, ("z", "yl"), blocks)
    both = lax.all_gather(half, "core", axis=0, tiled=True)
    near, far = both[: blocks * rows], both[blocks * rows :]
    hidden_part = jnp.dot(near, up_weight, preferred_element_type=jnp.float32)
    hidden_part = hidden_part + jnp.dot(far, up_other, preferred_element_type=jnp.float32)
    hidden_part = (hidden_part * LIFT).astype(jnp.float16).reshape(blocks, rows, shards)
    hidden_part, down_other = lax.optimization_barrier((hidden_part, down_other))
    hidden = jnp.sum(exchange(hidden_part, LIKE).astype(jnp.float32), axis=0) * (1.0 / LIFT)
    positive = jnp.maximum(hidden, 0.0)
    active = gather((positive * positive).astype(jnp.bfloat16), LIKE, blocks)
    mine = with_layout_constraint(jnp.dot(active, down_weight, preferred_element_type=jnp.float32), ROW_MAJOR)
    theirs = with_layout_constraint(jnp.dot(active, down_other, preferred_element_type=jnp.float32), ROW_MAJOR)
    swapped = lax.all_gather(jnp.where(same, theirs, mine).astype(jnp.bfloat16), "core", axis=0)
    other = jnp.where(first, swapped[1], swapped[0]).astype(jnp.float32)
    out_part = (jnp.where(same, mine, theirs) + other).astype(jnp.bfloat16).reshape(blocks, rows, width)
    mlp_out = jnp.sum(exchange(out_part, ("z", "yl")).astype(jnp.float32), axis=0)
    mlp_out = lax.ppermute(mlp_out, ("xh", "core"), [(0, 0), (1, 2), (2, 1), (3, 3)])
    combined = tokens.astype(jnp.float32) + keep_bits.astype(jnp.float32) * mlp_out / 0.9
    largest = lane_maxima(jnp.abs(combined))
    amax = jnp.max(max_over(max_over(largest, DP, n * lax.axis_size("yh")), TENSOR, 2 * blocks)).reshape(1)
    scaled = jnp.clip(combined * prior_scale[0], -448.0, 448.0).astype(jnp.bfloat16)
    return (scaled, amax)


def solution(mesh):
    fine = Mesh(mesh.devices.reshape(4, 2, 4, 8, 2, 2), DP + TENSOR)
    return jax.shard_map(
        body,
        mesh=fine,
        in_specs=(P(TENSOR, DP), P(DP, TENSOR), P(TENSOR, DP), P(TENSOR, DP), P()),
        out_specs=(P(TENSOR, DP), P()),
        check_vma=False,
    )
```

```python
import jax
import jax.numpy as jnp
from jax import lax
from jax.experimental.layout import Layout, with_layout_constraint
from jax.sharding import Mesh, PartitionSpec as P

DP = ("xp", "xh", "yh")
TENSOR = ("z", "yl", "core")
LIKE = ("xp", "yh")
LIFT = 64.0
ROW_MAJOR = Layout(major_to_minor=(0, 1))


def exchange(blocks, axes):
    return lax.all_to_all(blocks, axes, split_axis=0, concat_axis=0, tiled=True)


def gather(block, axes, n):
    spread = exchange(jnp.broadcast_to(block, (n,) + block.shape), axes)
    return spread.reshape((n * block.shape[0],) + block.shape[1:])


def max_over(values, axes, n):
    return jnp.max(exchange(jnp.broadcast_to(values, (n,) + values.shape), axes), axis=0)


def lane_maxima(values):
    lanes = 128
    tail = values.shape[1] % lanes
    largest = jnp.max(jnp.pad(values[:, values.shape[1] - tail :], ((0, 0), (0, lanes - tail))), axis=0)
    for low in range(0, values.shape[1] - tail, lanes):
        largest = jnp.maximum(largest, jnp.max(values[:, low : low + lanes], axis=0))
    return largest[None]


def partner(x, n):
    return (x + 1) % n if x % 2 else (x - 1) % n


def body(tokens, up_weight, down_weight, keep_bits, prior_scale):
    rows, width = tokens.shape
    shards = up_weight.shape[1]
    n = 2 * lax.axis_size("xp")
    blocks = lax.axis_size("z") * lax.axis_size("yl")
    core = lax.axis_index("core")
    first, same, tokens = lax.optimization_barrier((core == 0, core == lax.axis_index("xh"), tokens))
    moves = []
    for x in range(n):
        moves.append((2 * x + x % 2, 2 * x))
        moves.append((2 * x + 1 - x % 2, 2 * partner(x, n) + 1))
    up_other = lax.ppermute(up_weight, ("xp", "xh"), [(x, partner(x, n)) for x in range(n)])
    down_other = lax.ppermute(down_weight, "xh", [(0, 1), (1, 0)])
    chosen = lax.ppermute(tokens, ("xp", "xh", "core"), moves)
    half = gather(chosen, ("z", "yl"), blocks)
    both = lax.all_gather(half, "core", axis=0, tiled=True)
    near, far = both[: blocks * rows], both[blocks * rows :]
    hidden_part = jnp.dot(near, up_weight, preferred_element_type=jnp.float32)
    hidden_part = hidden_part + jnp.dot(far, up_other, preferred_element_type=jnp.float32)
    hidden_part = (hidden_part * LIFT).astype(jnp.float16).reshape(blocks, rows, shards)
    hidden_part, down_other = lax.optimization_barrier((hidden_part, down_other))
    hidden = jnp.sum(exchange(hidden_part, LIKE).astype(jnp.float32), axis=0) * (1.0 / LIFT)
    positive = jnp.maximum(hidden, 0.0)
    active = gather((positive * positive).astype(jnp.bfloat16), LIKE, blocks)
    mine = with_layout_constraint(jnp.dot(active, down_weight, preferred_element_type=jnp.float32), ROW_MAJOR)
    theirs = with_layout_constraint(jnp.dot(active, down_other, preferred_element_type=jnp.float32), ROW_MAJOR)
    swapped = lax.all_gather(jnp.where(same, theirs, mine).astype(jnp.bfloat16), "core", axis=0)
    other = jnp.where(first, swapped[1], swapped[0]).astype(jnp.float32)
    out_part = (jnp.where(same, mine, theirs) + other).astype(jnp.bfloat16).reshape(blocks, rows, width)
    mlp_out = jnp.sum(exchange(out_part, ("z", "yl")).astype(jnp.float32), axis=0)
    mlp_out = lax.ppermute(mlp_out, ("xh", "core"), [(0, 0), (1, 2), (2, 1), (3, 3)])
    combined = tokens.astype(jnp.float32) + keep_bits.astype(jnp.float32) * mlp_out / 0.9
    largest = lane_maxima(jnp.abs(combined))
    amax = jnp.max(max_over(max_over(largest, DP, n * lax.axis_size("yh")), TENSOR, 2 * blocks)).reshape(1)
    scaled = jnp.clip(combined * prior_scale[0], -448.0, 448.0).astype(jnp.bfloat16)
    return (scaled, amax)


def solution(mesh):
    fine = Mesh(mesh.devices.reshape(4, 2, 4, 8, 2, 2), DP + TENSOR)
    return jax.shard_map(
        body,
        mesh=fine,
        in_specs=(P(TENSOR, DP), P(DP, TENSOR), P(TENSOR, DP), P(TENSOR, DP), P()),
        out_specs=(P(TENSOR, DP), P()),
        check_vma=False,
    )
```

```python
import jax
import jax.numpy as jnp
from jax import lax
from jax.experimental.layout import Layout, with_layout_constraint
from jax.sharding import Mesh, PartitionSpec as P

DP = ("xp", "xh", "yh")
TENSOR = ("z", "yl", "core")
LIKE = ("xp", "yh")
LIFT = 128.0
ROW_MAJOR = Layout(major_to_minor=(0, 1))


def exchange(blocks, axes):
    return lax.all_to_all(blocks, axes, split_axis=0, concat_axis=0, tiled=True)


def gather(block, axes, n):
    spread = exchange(jnp.broadcast_to(block, (n,) + block.shape), axes)
    return spread.reshape((n * block.shape[0],) + block.shape[1:])


def max_over(values, axes, n):
    return jnp.max(exchange(jnp.broadcast_to(values, (n,) + values.shape), axes), axis=0)


def lane_maxima(values):
    lanes = 128
    tail = values.shape[1] % lanes
    largest = jnp.max(jnp.pad(values[:, values.shape[1] - tail :], ((0, 0), (0, lanes - tail))), axis=0)
    for low in range(0, values.shape[1] - tail, lanes):
        largest = jnp.maximum(largest, jnp.max(values[:, low : low + lanes], axis=0))
    return largest[None]


def body(tokens, up_weight, down_weight, keep_bits, prior_scale):
    rows, width = tokens.shape
    shards = up_weight.shape[1]
    blocks = lax.axis_size("z") * lax.axis_size("yl")
    core = lax.axis_index("core")
    first, same, tokens = lax.optimization_barrier((core == 0, core == lax.axis_index("xh"), tokens))
    down_other = lax.ppermute(down_weight, "xh", [(0, 1), (1, 0)])
    half = gather(tokens, ("z", "yl"), blocks)
    gathered = lax.all_gather(half, "core", axis=0, tiled=True)
    hidden_part = jnp.dot(gathered, up_weight, preferred_element_type=jnp.float32)
    hidden_part = (hidden_part * LIFT).astype(jnp.float16).reshape(2 * blocks, rows, shards)
    hidden_part, down_other = lax.optimization_barrier((hidden_part, down_other))
    hidden = jnp.sum(exchange(hidden_part, ("xh",) + LIKE).astype(jnp.float32), axis=0) * (1.0 / LIFT)
    positive = jnp.maximum(hidden, 0.0)
    active = gather((positive * positive).astype(jnp.bfloat16), LIKE, blocks)
    mine = with_layout_constraint(jnp.dot(active, down_weight, preferred_element_type=jnp.float32), ROW_MAJOR)
    theirs = with_layout_constraint(jnp.dot(active, down_other, preferred_element_type=jnp.float32), ROW_MAJOR)
    swapped = lax.all_gather(jnp.where(same, theirs, mine).astype(jnp.bfloat16), "core", axis=0)
    other = jnp.where(first, swapped[1], swapped[0]).astype(jnp.float32)
    out_part = (jnp.where(same, mine, theirs) + other).astype(jnp.bfloat16).reshape(blocks, rows, width)
    mlp_out = jnp.sum(exchange(out_part, ("z", "yl")).astype(jnp.float32), axis=0)
    mlp_out = lax.ppermute(mlp_out, ("xh", "core"), [(0, 0), (1, 2), (2, 1), (3, 3)])
    combined = tokens.astype(jnp.float32) + keep_bits.astype(jnp.float32) * mlp_out / 0.9
    largest = lane_maxima(jnp.abs(combined))
    amax = jnp.max(max_over(max_over(largest, DP, 2 * blocks), TENSOR, 2 * blocks)).reshape(1)
    scaled = jnp.clip(combined * prior_scale[0], -448.0, 448.0).astype(jnp.bfloat16)
    return (scaled, amax)


def solution(mesh):
    fine = Mesh(mesh.devices.reshape(4, 2, 4, 8, 2, 2), DP + TENSOR)
    return jax.shard_map(
        body,
        mesh=fine,
        in_specs=(P(TENSOR, DP), P(DP, TENSOR), P(TENSOR, DP), P(TENSOR, DP), P()),
        out_specs=(P(TENSOR, DP), P()),
        check_vma=False,
    )
```
